256 devices in a mesh: dp: 8 (over z_hi, y), fsdp: 32 (over z_lo, x, core).
Axes of the slice: x: 4, y: 4, z: 8 (z_hi: 2, z_lo: 4; z = z_hi * 4 + z_lo), core: 2. Of those that a mesh axis runs over, the one named last changes fastest.
Arguments:
- clip_tokens: bfloat16 [5120, 4096], P('dp', 'fsdp'), may hold values from -6 to 6
- action_ids: int32 [8, 5], P('dp'), may hold values from 0 to 511
- token_counts: int32 [8], P('dp'), may hold values from 160 to 640, as said below
- action_table: bfloat16 [512, 4096], P(None, 'fsdp'), may hold values from -6 to 6
- norm_gain: float32 [3, 4096], replicated, may hold values from 0.5 to 1.5
- layer_weight: bfloat16 [3, 4096, 4096], P(None, None, 'fsdp'), may hold values from -0.09375 to 0.09375
- in_factor: bfloat16 [3, 64, 4096], P(None, None, 'fsdp'), may hold values from -0.09375 to 0.09375
- out_factor: bfloat16 [3, 64, 4096], P(None, None, 'fsdp'), may hold values from -0.09375 to 0.09375
- query_grads: bfloat16 [3, 2048, 4096], P(None, 'dp', 'fsdp'), may hold values from -0.001953125 to 0.001953125
- target: bfloat16 [5120, 4096], P('dp', 'fsdp'), may hold values from -6 to 6
Outputs:
- scores: float32 [8, 2048], P('dp', 'fsdp')
The draws below stay inside these ranges and needn't reach their ends.
Inputs may be any that keep to these rules, and one draw needn't show every extreme that they name: `token_counts`: the first clip has all 640 tokens live.
All inputs are finite; a program needn't handle non-finite values.
Results may differ from the reference program's by a relative error of at most 0.015.
Values may be sent and summed in bfloat16 or wider, within the bound.
No kernel may reach another device: no remote copies, remote signals or barrier semaphores. Data moves between devices by JAX's collectives and lax.ppermute only.
A program may use at most 128 MiB of HBM per device.

```python
import jax
import jax.numpy as jnp
from jax import lax

D = 4096
K = 64
NQ = 2048
LAYERS = 3
FRAMES = 5
TPF = 128
ACTIONS = 512
TOKC = 640
CLIPS = 8
N_FSDP = 32


def draw_token_counts(key, part):
    key = jax.random.fold_in(key, 11)
    counts = jax.random.randint(key, (CLIPS,), TOKC // 4, TOKC + 1)
    return counts.at[0].set(TOKC).astype(jnp.int32)


def place_ends(values, rng, low, top_value):
    index_at = [jax.random.randint(jax.random.fold_in(rng, axis), (), 0, length) for axis, length in enumerate(values.shape)]
    main_axis = values.shape.index(max(values.shape))
    next_to = index_at[:main_axis] + [(index_at[main_axis] + 1) % values.shape[main_axis]] + index_at[main_axis + 1:]
    return values.at[tuple(index_at)].set(low).at[tuple(next_to)].set(top_value)


def levels(rng, shape, cuts, least, top_value):
    def one(axis_at, blocks):
        steps = jax.random.uniform(jax.random.fold_in(jax.random.fold_in(rng, 6), axis_at), (blocks,), jnp.float32, least / len(cuts), top_value / len(cuts))
        return jnp.repeat(jnp.exp(steps), shape[axis_at] // blocks).reshape((-1,) + (1,) * (len(shape) - axis_at - 1))

    level = one(*cuts[0])
    for cut in cuts[1:]:
        level = level * one(*cut)
    return level


def gaussian(key, shape, spread, bound, split=(), dtype=jnp.bfloat16):
    loudness = levels(key, shape, split, -0.22, 0.18) if split else 1.0
    array = jax.random.normal(key, shape, jnp.float32) * spread * loudness
    return jnp.minimum(jnp.maximum(array, -bound), bound).astype(dtype)


def setup_inputs(seed: int = 0) -> dict:
    streams_of = jax.random.split(jax.random.key(seed), 11)
    return {
        "clip_tokens": gaussian(streams_of[0], (CLIPS * TOKC, D), 1.0, 6.0, ((0, 8), (1, 32))),
        "action_ids": place_ends(jax.random.randint(streams_of[1], (CLIPS, FRAMES), 0, ACTIONS), jax.random.fold_in(streams_of[1], 1), 0, ACTIONS - 1).astype(jnp.int32),
        "token_counts": draw_token_counts(jax.random.fold_in(streams_of[10], 71), 0),
        "action_table": gaussian(streams_of[3], (ACTIONS, D), 1.0, 6.0, ((1, 32),)),
        "norm_gain": jnp.clip(1.0 + 0.1 * jax.random.normal(streams_of[4], (LAYERS, D), jnp.float32), 0.5, 1.5),
        "layer_weight": gaussian(streams_of[5], (LAYERS, D, D), D ** -0.5, 0.09375, ((2, 32),)),
        "in_factor": gaussian(streams_of[6], (LAYERS, K, D), D ** -0.5, 0.09375, ((2, 32),)),
        "out_factor": gaussian(streams_of[7], (LAYERS, K, D), D ** -0.5, 0.09375, ((2, 32),)),
        "query_grads": gaussian(streams_of[8], (LAYERS, NQ, K * K), (TOKC * LAYERS * K * K) ** -0.5, 0.001953125, ((1, 8), (2, 32))),
        "target": gaussian(streams_of[9], (CLIPS * TOKC, D), 1.0, 6.0, ((0, 8), (1, 32))),
    }


EPS = 1e-06

def silu_grad(value):
    sig = jax.nn.sigmoid(value)
    return sig * (1.0 + value * (1.0 - sig))

def block_product(grads, weight):
    count = grads.shape[0]
    width = weight.shape[1] // N_FSDP
    grad_blocks = grads.reshape(count, N_FSDP, width).transpose(1, 0, 2)
    weight_blocks = weight.reshape(weight.shape[0], N_FSDP, width).transpose(1, 0, 2)

    def add_block(total, pair):
        term = jnp.dot(pair[0], pair[1].T, preferred_element_type=jnp.float32).astype(jnp.bfloat16)
        term = lax.optimization_barrier(term)
        return (total + term.astype(jnp.float32), None)
    start = jnp.zeros((count, weight.shape[0]), jnp.float32)
    total, unused = lax.scan(add_block, start, (grad_blocks, weight_blocks))
    return total

def reference(clip_tokens, action_ids, token_counts, action_table, norm_gain, layer_weight, in_factor, out_factor, query_grads, target):
    rows = CLIPS * TOKC
    frame_of = jnp.arange(TOKC) // TPF
    acts = action_ids[:, frame_of].reshape(rows)
    onehot = (acts[:, None] == jnp.arange(ACTIONS)[None, :]).astype(jnp.bfloat16)
    embed = jnp.dot(onehot, action_table, preferred_element_type=jnp.float32)
    state = (clip_tokens.astype(jnp.float32) + embed).astype(jnp.bfloat16)
    saved = []
    for layer in range(LAYERS):
        hfull = state.astype(jnp.float32)
        ratio = lax.rsqrt(lax.optimization_barrier(jnp.mean(hfull * hfull, axis=1, keepdims=True)) + EPS)
        normed = (hfull * ratio * norm_gain[layer]).astype(jnp.bfloat16)
        pre = jnp.dot(normed, layer_weight[layer], preferred_element_type=jnp.float32)
        saved.append((hfull, ratio, normed, pre))
        state = (hfull + jax.nn.silu(pre)).astype(jnp.bfloat16)
    live = (jnp.arange(TOKC)[None, :] < token_counts[:, None]).reshape(rows, 1)
    delta = jnp.where(live, state.astype(jnp.float32) - target.astype(jnp.float32), 0.0)
    scores = jnp.zeros((CLIPS, NQ), jnp.float32)
    for layer in range(LAYERS - 1, -1, -1):
        hfull, ratio, normed, pre = saved[layer]
        egrad = (delta * silu_grad(pre)).astype(jnp.bfloat16)
        pfac = jnp.dot(normed, in_factor[layer].T, preferred_element_type=jnp.float32)
        qfac = jnp.dot(egrad, out_factor[layer].T, preferred_element_type=jnp.float32)
        outer = jnp.einsum('ctk,ctj->ckj', pfac.reshape(CLIPS, TOKC, K), qfac.reshape(CLIPS, TOKC, K))
        outer = outer.reshape(CLIPS, K * K).astype(jnp.bfloat16)
        scores = scores + jnp.dot(outer, query_grads[layer].T, preferred_element_type=jnp.float32)
        if layer > 0:
            back = block_product(egrad, layer_weight[layer])
            gain = norm_gain[layer]
            mean_term = lax.optimization_barrier(jnp.mean(back * gain * hfull, axis=1, keepdims=True))
            delta = delta + ratio * gain * back - hfull * ratio ** 3 * mean_term
    return scores
```

```python
import functools

import jax
import jax.numpy as jnp
from jax import lax
from jax.experimental import pallas as pl
from jax.experimental.pallas import tpu as pltpu
from jax.sharding import Mesh, PartitionSpec as P

EPS = 1e-06
BF = jnp.bfloat16
F32 = jnp.float32
LANE = 128
VLIMIT = 48 * 1024 * 1024


def any_spec():
    return pl.BlockSpec(memory_space=pl.ANY)


def vmem():
    return pl.BlockSpec(memory_space=pltpu.VMEM)


def smem():
    return pl.BlockSpec(memory_space=pltpu.SMEM)


def feature(zz, xx, cc):
    return pl.multiple_of(zz * 1024 + xx * 256 + cc * LANE, LANE)


SLOT_Z = (0, 3, 1, 2)


def load_weight(places, refs, wbuf, sems):
    copies = []
    for n, (place, ref) in enumerate(zip(places, refs)):
        layer, slot, row, core = place
        src = ref if layer is None else ref.at[layer]
        rows = src.shape[0]
        copy = pltpu.make_async_copy(
            src, wbuf.at[slot, pl.ds(row, rows), pl.ds(core * LANE, LANE)], sems.at[n]
        )
        copy.start()
        copies.append((slot, copy))
    return copies


def wait_slot(copies, slot):
    for where, copy in copies:
        if where == slot:
            copy.wait()


def block_of(meta, slot, core):
    zz = lax.rem(meta[0] + SLOT_Z[slot], 4)
    cc = meta[2] if core == 0 else 1 - meta[2]
    return zz * 2 + cc


def sigm(v):
    return 1.0 / (1.0 + jnp.exp(-v))


def norm_rows(meta, layer, blocks, gain, hfull, ubuf, width):
    total = None
    for k, ref in enumerate(blocks):
        xx = lax.rem(meta[1] + 4 - k, 4)
        for j in range(8):
            block = ref[j]
            hfull[:, pl.ds(feature(j // 2, xx, j % 2), LANE)] = block
            value = block.astype(F32)
            total = value * value if total is None else total + value * value
    ratio = lax.rsqrt(jnp.sum(total, axis=1, keepdims=True) / width + EPS)
    for n in range(width // 256):
        cols = slice(n * 256, n * 256 + 256)
        ubuf[:, cols] = (hfull[:, cols].astype(F32) * ratio * gain[layer : layer + 1, cols]).astype(BF)
    return ratio


def forward_body(meta, layer, places, blocks, gain, wrefs, hfull, rout, uown, aout, wbuf, ubuf, sems, width, finish):
    copies = load_weight(places, wrefs, wbuf, sems)
    ratio = norm_rows(meta, layer, blocks, gain, hfull, ubuf, width)
    rout[...] = jnp.broadcast_to(ratio, rout.shape)
    for j in range(8):
        uown[j] = ubuf[:, pl.ds(feature(j // 2, meta[1], j % 2), LANE)]
    for slot in range(4):
        wait_slot(copies, slot)
        pre = jnp.dot(ubuf[...], wbuf[slot], preferred_element_type=F32)
        for core in range(2):
            value = pre[:, core * LANE : core * LANE + LANE]
            j = block_of(meta, slot, core)
            aout[j] = value
            finish(j, value)
    return ratio


def forward_kernel(layer, places, width, meta, h0, h1, h2, h3, gain, *rest):
    n = len(places)
    wrefs = rest[:n]
    hnew, aout, uown, hfull, rout, wbuf, ubuf, sems = rest[n:]

    def finish(j, value):
        hnew[j] = (h0[j].astype(F32) + value * sigm(value)).astype(BF)

    forward_body(
        meta, layer, places, (h0, h1, h2, h3), gain, wrefs, hfull, rout, uown, aout, wbuf, ubuf, sems, width, finish
    )


def back_product(meta, layer, aref, eout, hfull, ratio, gain, wbuf, outs, width):
    dot_sum = None
    for j in range(8):
        term = eout[j].astype(F32) * aref[j]
        dot_sum = term if dot_sum is None else dot_sum + term
    scale = ratio * ratio * (jnp.sum(dot_sum, axis=1, keepdims=True) / width)
    grads = []
    for slot in range(4):
        grads.append(
            jnp.concatenate([eout[block_of(meta, slot, 0)], eout[block_of(meta, slot, 1)]], axis=1)
        )
    for k, out in enumerate(outs):
        xx = lax.rem(meta[1] + k, 4)
        for zz in range(4):
            first = pl.multiple_of(zz * 1024 + xx * 256, 256)
            acc = None
            for slot in range(4):
                part = lax.dot_general(
                    grads[slot],
                    wbuf[slot, pl.ds(first, 256), :],
                    (((1,), (1,)), ((), ())),
                    preferred_element_type=F32,
                )
                acc = part if acc is None else acc + part
            value = ratio * gain[layer : layer + 1, pl.ds(first, 256)] * acc - scale * hfull[
                :, pl.ds(first, 256)
            ].astype(F32)
            for cc in range(2):
                out[zz * 2 + cc] = value[:, cc * LANE : cc * LANE + LANE].astype(out.dtype)


def grad_of(delta, value):
    sig = sigm(value)
    return (delta * (sig * (1.0 + value * (1.0 - sig)))).astype(BF)


def turn_kernel(layer, places, width, meta, h0, h1, h2, h3, gain, target, *rest):
    n = len(places)
    wrefs = rest[:n]
    uown, delta, eout, o0, o1, o2, o3, hfull, rout, aout, wbuf, ubuf, sems = rest[n:]
    rows = h0.shape[1]
    token = (meta[0] * 2 + meta[2]) * rows + lax.broadcasted_iota(jnp.int32, (rows, 1), 0)
    live = token < meta[3]

    def finish(j, value):
        hlast = (h0[j].astype(F32) + value * sigm(value)).astype(BF)
        grad = jnp.where(live, hlast.astype(F32) - target[j].astype(F32), 0.0)
        delta[j] = grad
        eout[j] = grad_of(grad, value)

    ratio = forward_body(
        meta, layer, places, (h0, h1, h2, h3), gain, wrefs, hfull, rout, uown, aout, wbuf, ubuf, sems, width, finish
    )
    back_product(meta, layer, aout, eout, hfull, ratio, gain, wbuf, (o0, o1, o2, o3), width)


def back_kernel(layer, places, width, meta, din, i0, i1, i2, i3, aref, hfull, rref, gain, *rest):
    n = len(places)
    wrefs = rest[:n]
    delta, eout, o0, o1, o2, o3, wbuf, sems = rest[n:]
    copies = load_weight(places, wrefs, wbuf, sems)
    for j in range(8):
        grad = din[j] + i0[j] + i1[j].astype(F32) + i2[j].astype(F32) + i3[j].astype(F32)
        delta[j] = grad
        eout[j] = grad_of(grad, aref[j])
    for slot in range(4):
        wait_slot(copies, slot)
    back_product(meta, layer, aref, eout, hfull, rref[:, 0:1], gain, wbuf, (o0, o1, o2, o3), width)


def dot_t(left, right):
    return lax.dot_general(left, right, (((1,), (1,)), ((), ())), preferred_element_type=F32)


def inner_kernel(u0, u1, u2, factors, out):
    for layer, ref in enumerate((u0, u1, u2)):
        acc = None
        for j in range(8):
            part = dot_t(ref[j], factors[j, layer, 0:64, :])
            acc = part if acc is None else acc + part
        out[:, layer * 64 : layer * 64 + 64] = acc.astype(BF)
    out[:, 192:256] = jnp.zeros((out.shape[0], 64), BF)


def project(eref, factors, layer):
    acc = None
    for j in range(8):
        part = dot_t(eref[j], factors[j, layer, 64:128, :])
        acc = part if acc is None else acc + part
    return acc


def outer(left, right):
    full = lax.dot_general(
        left, right, (((0,), (0,)), ((), ())), preferred_element_type=F32, precision=lax.Precision.HIGHEST
    )
    return jnp.concatenate([full[:32], full[32:]], axis=1)


def outer_kernel(e1, e2, p0, p1, p2, p3, factors, pout, gout):
    psum = p0[...].astype(F32) + p1[...].astype(F32) + p2[...].astype(F32) + p3[...].astype(F32)
    pout[...] = psum
    for n, (layer, ref) in enumerate(((1, e1), (2, e2))):
        q = project(ref, factors, layer)
        gout[:, n * LANE : n * LANE + LANE] = outer(psum[:, layer * 64 : layer * 64 + 64], q)


def last_kernel(din, i0, i1, i2, i3, aref, factors, pref, gin, out, eout):
    for j in range(8):
        grad = din[j] + i0[j] + i1[j].astype(F32) + i2[j].astype(F32) + i3[j].astype(F32)
        eout[j] = grad_of(grad, aref[j])
    q = project(eout, factors, 0)
    out[:, 0:LANE] = outer(pref[:, 0:64], q)
    out[:, LANE:] = gin[...]


def embed_kernel(ids, clip, table, target, out, rows_buf):
    frames = ids.shape[1]
    per = clip.shape[0] // frames
    rows = out.shape[1]
    for f in range(frames):
        group = pl.multiple_of((ids[0, f] // 16) * 16, 16)
        at = ids[0, f] - group
        tile = table[pl.ds(group, 16), :].astype(F32)
        pick = lax.broadcasted_iota(jnp.int32, (16, 1), 0) == at
        row = jnp.sum(jnp.where(pick, tile, 0.0), axis=0, keepdims=True)
        rows_buf[f * per : f * per + per, :] = (clip[f * per : f * per + per, :].astype(F32) + row).astype(BF)
    for n in range(out.shape[0]):
        out[n, :, 0:LANE] = rows_buf[n * rows : n * rows + rows, :]
        out[n, :, LANE:] = target[n * rows : n * rows + rows, :]


def call(kernel, out_shape, in_specs, scratch, flops, moved, name, *args):
    many = isinstance(out_shape, (tuple, list))
    return pl.pallas_call(
        kernel,
        out_shape=out_shape,
        in_specs=in_specs,
        out_specs=[vmem() for _ in out_shape] if many else vmem(),
        scratch_shapes=scratch,
        compiler_params=pltpu.CompilerParams(vmem_limit_bytes=VLIMIT),
        cost_estimate=pl.CostEstimate(flops=flops, bytes_accessed=moved, transcendentals=0),
        name=name,
    )(*args)


def ring(x, axes, size, k):
    return lax.ppermute(x, axes, [(i, (i + k) % size) for i in range(size)])


def swap(x):
    return lax.ppermute(x, "c", [(0, 1), (1, 0)])


def zring(x, k):
    return ring(x, ("zh", "z"), 8, k)


def spread(x):
    return [x] + [ring(x, "x", 4, k) for k in (1, 2, 3)]


def gather_weight(layer_weight, layer):
    own = layer_weight[layer]
    half = own.shape[0] // 2
    right = zring(own, 1)
    left = zring(own, -1)
    right2 = zring(right[:half], 1)
    left2 = zring(left[half:], -1)
    pieces = [
        (layer_weight, layer, 0, 0, 0),
        (right, None, 1, 0, 0),
        (left, None, 2, 0, 0),
        (right2, None, 3, 0, 0),
        (left2, None, 3, half, 0),
    ]
    pieces += [(swap(own), None, 0, 0, 1)]
    pieces += [(swap(arr), None, slot, row, 1) for arr, _, slot, row, _ in pieces[1:5]]
    return [p[0] for p in pieces], [p[1:] for p in pieces]


def local(
    clip_tokens,
    action_ids,
    token_counts,
    action_table,
    norm_gain,
    layer_weight,
    in_factor,
    out_factor,
    query_grads,
    target,
):
    width = norm_gain.shape[1]
    rows = clip_tokens.shape[0] // 8
    meta = jnp.stack(
        [lax.axis_index("z"), lax.axis_index("x"), lax.axis_index("c"), token_counts[0]]
    ).astype(jnp.int32)
    block = lambda dtype: jax.ShapeDtypeStruct((8, rows, LANE), dtype)
    whole = jax.ShapeDtypeStruct((rows, width), BF)
    ratio_shape = jax.ShapeDtypeStruct((rows, LANE), F32)
    flops = 2 * rows * width * 1024
    moved = width * 1024 * 2

    start = call(
        embed_kernel,
        jax.ShapeDtypeStruct((8, rows, 2 * LANE), BF),
        [smem(), vmem(), vmem(), vmem()],
        [pltpu.VMEM((8 * rows, LANE), BF)],
        10**6,
        10**6,
        "embed",
        action_ids,
        clip_tokens,
        action_table,
        target,
    )
    weights = [gather_weight(layer_weight, layer) for layer in range(3)]
    start = lax.all_to_all(start, ("z", "c"), 0, 0)
    state = start[:, :, :LANE]
    goal = start[:, :, LANE:]

    order = jnp.concatenate([in_factor[:, 0::2], in_factor[:, 1::2], out_factor], axis=1)
    factors = lax.all_gather(order, ("z", "c"))
    queries = lax.all_gather(query_grads, ("zh", "y"), axis=1, tiled=True)

    def wscratch(n):
        return [pltpu.VMEM((4, width, 256), BF)], [pltpu.SemaphoreType.DMA((n,))]

    saved = []
    for layer in range(2):
        arrays, places = weights[layer]
        wb, sems = wscratch(len(places))
        blocks = spread(state)
        state, pre, uown, hfull, ratio = call(
            functools.partial(forward_kernel, layer, places, width),
            [block(BF), block(F32), block(BF), whole, ratio_shape],
            [smem()] + [vmem()] * 5 + [any_spec()] * len(places),
            wb + [pltpu.VMEM((rows, width), BF)] + sems,
            flops,
            moved,
            "forward%d" % layer,
            meta,
            *blocks,
            norm_gain,
            *arrays,
        )
        saved.append((pre, uown, hfull, ratio))

    arrays, places = weights[2]
    wb, sems = wscratch(len(places))
    blocks = spread(state)
    u2, delta, e2, *parts = call(
        functools.partial(turn_kernel, 2, places, width),
        [block(BF), block(F32), block(BF), block(F32), block(BF), block(BF), block(BF)],
        [smem()] + [vmem()] * 6 + [any_spec()] * len(places),
        [pltpu.VMEM((rows, width), BF), pltpu.VMEM((rows, LANE), F32), pltpu.VMEM((8, rows, LANE), F32)]
        + wb
        + [pltpu.VMEM((rows, width), BF)]
        + sems,
        2 * flops,
        moved,
        "turn",
        meta,
        *blocks,
        norm_gain,
        goal,
        *arrays,
    )

    def scatter(parts):
        return [parts[0]] + [ring(parts[k], "x", 4, k) for k in (1, 2, 3)]

    incs = scatter(parts)
    inner = call(
        inner_kernel,
        jax.ShapeDtypeStruct((rows, 256), BF),
        [vmem()] * 4,
        [],
        10**7,
        10**6,
        "inner",
        saved[0][1],
        saved[1][1],
        u2,
        factors,
    )
    inners = spread(inner)

    arrays, places = weights[1]
    wb, sems = wscratch(len(places))
    pre, _, hfull, ratio = saved[1]
    delta, e1, *parts = call(
        functools.partial(back_kernel, 1, places, width),
        [block(F32), block(BF), block(F32), block(BF), block(BF), block(BF)],
        [smem()] + [vmem()] * 9 + [any_spec()] * len(places),
        wb + sems,
        flops,
        moved,
        "back1",
        meta,
        delta,
        *incs,
        pre,
        hfull,
        ratio,
        norm_gain,
        *arrays,
    )
    incs = scatter(parts)
    pfull, gpart = call(
        outer_kernel,
        [jax.ShapeDtypeStruct((rows, 256), F32), jax.ShapeDtypeStruct((32, 256), F32)],
        [vmem()] * 7,
        [],
        10**7,
        10**6,
        "outer",
        e1,
        e2,
        *inners,
        factors,
    )
    gall = call(
        last_kernel,
        jax.ShapeDtypeStruct((32, 384), F32),
        [vmem()] * 9,
        [pltpu.VMEM((8, rows, LANE), BF)],
        10**7,
        10**6,
        "last",
        delta,
        *incs,
        saved[0][0],
        factors,
        pfull,
        gpart,
    )
    everyone = ("z", "x", "c")
    gmine = jnp.sum(lax.all_to_all(gall, everyone, 0, 0, tiled=True), axis=0).astype(BF)
    partial = jnp.einsum(
        "lk,lqk->q", gmine.reshape(3, LANE), queries, preferred_element_type=F32
    )
    mine = lax.all_to_all(partial.reshape(32, partial.shape[0] // 32), everyone, 0, 0, tiled=True)
    return jnp.sum(mine, axis=0, keepdims=True)


def solution(mesh):
    fine = Mesh(mesh.devices.reshape(2, 4, 4, 4, 2), ("zh", "y", "z", "x", "c"))
    dp = ("zh", "y")
    fsdp = ("z", "x", "c")
    return jax.shard_map(
        local,
        mesh=fine,
        in_specs=(
            P(dp, fsdp),
            P(dp, None),
            P(dp),
            P(None, fsdp),
            P(),
            P(None, None, fsdp),
            P(None, None, fsdp),
            P(None, None, fsdp),
            P(None, dp, fsdp),
            P(dp, fsdp),
        ),
        out_specs=P(dp, fsdp),
        check_vma=False,
    )
```

```python
import functools

import jax
import jax.numpy as jnp
from jax import lax
from jax.experimental import pallas as pl
from jax.experimental.pallas import tpu as pltpu
from jax.sharding import Mesh, PartitionSpec as P

EPS = 1e-06
BF = jnp.bfloat16
F32 = jnp.float32
LANE = 128
VLIMIT = 20 * 1024 * 1024


def hbm():
    return pl.BlockSpec(memory_space=pltpu.HBM)


def vmem():
    return pl.BlockSpec(memory_space=pltpu.VMEM)


def smem():
    return pl.BlockSpec(memory_space=pltpu.SMEM)


def feature(zz, xx, cc):
    return pl.multiple_of(zz * 1024 + xx * 256 + cc * LANE, LANE)


SLOT_Z = (0, 3, 1, 2)


def load_weight(meta, places, refs, wbuf, sems):
    copies = []
    for n, (place, ref) in enumerate(zip(places, refs)):
        index, first, rows, slot, row, core = place
        if index is None:
            src = ref
        elif isinstance(index, int):
            src = ref.at[index]
        else:
            owner = meta[2] if core == 0 else 1 - meta[2]
            src = ref.at[index[1] * 2 + owner, slot]
        copy = pltpu.make_async_copy(
            src.at[pl.ds(first, rows)],
            wbuf.at[slot, pl.ds(row, rows), pl.ds(core * LANE, LANE)],
            sems.at[n],
        )
        copy.start()
        copies.append((slot, copy))
    return copies


def wait_slot(copies, slot):
    for where, copy in copies:
        if where == slot:
            copy.wait()


def block_of(meta, slot, core):
    zz = lax.rem(meta[0] + SLOT_Z[slot], 4)
    cc = meta[2] if core == 0 else 1 - meta[2]
    return zz * 2 + cc


def sigm(v):
    return 1.0 / (1.0 + jnp.exp(-v))


def norm_rows(meta, layer, blocks, gain, hfull, ubuf, width):
    total = None
    for k, ref in enumerate(blocks):
        xx = lax.rem(meta[1] + 4 - k, 4)
        for j in range(8):
            block = ref[j]
            hfull[:, pl.ds(feature(j // 2, xx, j % 2), LANE)] = block
            value = block.astype(F32)
            total = value * value if total is None else total + value * value
    ratio = lax.rsqrt(jnp.sum(total, axis=1, keepdims=True) / width + EPS)
    for n in range(width // 256):
        cols = slice(n * 256, n * 256 + 256)
        ubuf[:, cols] = (hfull[:, cols].astype(F32) * ratio * gain[layer : layer + 1, cols]).astype(BF)
    return ratio


def forward_body(meta, layer, places, blocks, gain, wrefs, hfull, rout, uown, aout, wbuf, ubuf, sems, width, finish):
    copies = load_weight(meta, places, wrefs, wbuf, sems)
    ratio = norm_rows(meta, layer, blocks, gain, hfull, ubuf, width)
    rout[...] = jnp.broadcast_to(ratio, rout.shape)
    for j in range(8):
        uown[j] = ubuf[:, pl.ds(feature(j // 2, meta[1], j % 2), LANE)]
    for slot in range(4):
        wait_slot(copies, slot)
        pre = jnp.dot(ubuf[...], wbuf[slot, 0:width, :], preferred_element_type=F32)
        for core in range(2):
            value = pre[:, core * LANE : core * LANE + LANE]
            j = block_of(meta, slot, core)
            aout[j] = value
            finish(j, value)
    return ratio


def forward_kernel(layer, places, width, meta, h0, h1, h2, h3, gain, *rest):
    n = len(places)
    wrefs = rest[:n]
    hnew, aout, uown, hfull, rout, wbuf, ubuf, sems = rest[n:]

    def finish(j, value):
        hnew[j] = (h0[j].astype(F32) + value * sigm(value)).astype(BF)

    forward_body(
        meta, layer, places, (h0, h1, h2, h3), gain, wrefs, hfull, rout, uown, aout, wbuf, ubuf, sems, width, finish
    )


def back_product(meta, layer, aref, eout, hfull, ratio, gain, wbuf, outs, width):
    dot_sum = None
    for j in range(8):
        term = eout[j].astype(F32) * aref[j]
        dot_sum = term if dot_sum is None else dot_sum + term
    scale = ratio * ratio * (jnp.sum(dot_sum, axis=1, keepdims=True) / width)
    grads = []
    for slot in range(4):
        grads.append(
            jnp.concatenate([eout[block_of(meta, slot, 0)], eout[block_of(meta, slot, 1)]], axis=1)
        )
    for k, out in enumerate(outs):
        xx = lax.rem(meta[1] + k, 4)
        for zz in range(4):
            first = pl.multiple_of(zz * 1024 + xx * 256, 256)
            acc = None
            for slot in range(4):
                part = lax.dot_general(
                    grads[slot],
                    wbuf[slot, pl.ds(first, 256), :],
                    (((1,), (1,)), ((), ())),
                    preferred_element_type=F32,
                )
                acc = part if acc is None else acc + part
            value = ratio * gain[layer : layer + 1, pl.ds(first, 256)] * acc - scale * hfull[
                :, pl.ds(first, 256)
            ].astype(F32)
            for cc in range(2):
                out[zz * 2 + cc] = value[:, cc * LANE : cc * LANE + LANE].astype(out.dtype)


def grad_of(delta, value):
    sig = sigm(value)
    return (delta * (sig * (1.0 + value * (1.0 - sig)))).astype(BF)


def factor_rows(width, layer, which):
    first = width + (layer * 2 + which) * 64
    return slice(first, first + 64)


def slot_pair(meta, ref, slot):
    return jnp.concatenate([ref[block_of(meta, slot, 0)], ref[block_of(meta, slot, 1)]], axis=1)


def turn_kernel(layer, places, width, meta, h0, h1, h2, h3, gain, target, u0, u1, *rest):
    n = len(places)
    wrefs = rest[:n]
    delta, pout, qout, fout, o0, o1, o2, o3, eout, uown, hfull, rout, aout, wbuf, ubuf, sems = rest[n:]
    rows = h0.shape[1]
    token = (meta[0] * 2 + meta[2]) * rows + lax.broadcasted_iota(jnp.int32, (rows, 1), 0)
    live = token < meta[3]

    def finish(j, value):
        hlast = (h0[j].astype(F32) + value * sigm(value)).astype(BF)
        grad = jnp.where(live, hlast.astype(F32) - target[j].astype(F32), 0.0)
        delta[j] = grad
        eout[j] = grad_of(grad, value)

    ratio = forward_body(
        meta, layer, places, (h0, h1, h2, h3), gain, wrefs, hfull, rout, uown, aout, wbuf, ubuf, sems, width, finish
    )
    back_product(meta, layer, aout, eout, hfull, ratio, gain, wbuf, (o0, o1, o2, o3), width)
    for at, ref in enumerate((u0, u1, uown)):
        acc = None
        for slot in range(4):
            part = dot_t(slot_pair(meta, ref, slot), wbuf[slot, factor_rows(width, at, 0), :])
            acc = part if acc is None else acc + part
        lanes = slice(at % 2 * 64, at % 2 * 64 + 64)
        pout[at // 2, :, lanes] = acc
        for out in (o1, o2, o3):
            out[8 + at // 2, :, lanes] = acc.astype(BF)
    for out in (o1, o2, o3):
        out[9, :, 64:] = jnp.zeros((rows, 64), BF)
    pout[1, :, 64:] = jnp.zeros((rows, 64), F32)
    acc = None
    for slot in range(4):
        part = dot_t(slot_pair(meta, eout, slot), wbuf[slot, factor_rows(width, 2, 1), :])
        acc = part if acc is None else acc + part
        for at in range(2):
            fout[at, slot] = wbuf[slot, factor_rows(width, at, 1), :]
    qout[...] = acc


def project(meta, eref, fref, layer):
    acc = None
    for slot in range(4):
        part = dot_t(slot_pair(meta, eref, slot), fref[layer, slot])
        acc = part if acc is None else acc + part
    return acc


def back_kernel(layer, places, width, meta, din, i0, i1, i2, i3, aref, hfull, rref, gain, fref, pin, q2, *rest):
    n = len(places)
    wrefs = rest[:n]
    delta, pout, gout, o0, o1, o2, o3, eout, wbuf, sems = rest[n:]
    copies = load_weight(meta, places, wrefs, wbuf, sems)
    for j in range(8):
        grad = din[j] + i0[j] + i1[j].astype(F32) + i2[j].astype(F32) + i3[j].astype(F32)
        delta[j] = grad
        eout[j] = grad_of(grad, aref[j])
    for slot in range(4):
        wait_slot(copies, slot)
    back_product(meta, layer, aref, eout, hfull, rref[:, 0:1], gain, wbuf, (o0, o1, o2, o3), width)
    psum = [
        pin[n] + i1[8 + n].astype(F32) + i2[8 + n].astype(F32) + i3[8 + n].astype(F32) for n in range(2)
    ]
    pout[...] = psum[0][:, 0:64]
    gout[:, 0:LANE] = outer(psum[0][:, 64:LANE], project(meta, eout, fref, 1))
    gout[:, LANE:] = outer(psum[1][:, 0:64], q2[...])


def dot_t(left, right):
    return lax.dot_general(left, right, (((1,), (1,)), ((), ())), preferred_element_type=F32)


def outer(left, right):
    full = lax.dot_general(
        left, right, (((0,), (0,)), ((), ())), preferred_element_type=F32, precision=lax.Precision.HIGHEST
    )
    return jnp.concatenate([full[:32], full[32:]], axis=1)


def last_kernel(meta, din, i0, i1, i2, i3, aref, fref, pref, gin, out, eout):
    for j in range(8):
        grad = din[j] + i0[j] + i1[j].astype(F32) + i2[j].astype(F32) + i3[j].astype(F32)
        eout[j] = grad_of(grad, aref[j])
    out[:, 0:LANE] = outer(pref[...], project(meta, eout, fref, 0))
    out[:, LANE:] = gin[...]


def score_kernel(spot, gall, q0, q1, q2, q3, out):
    grads = jnp.sum(gall[...], axis=0, keepdims=True).astype(BF)
    for k, ref in enumerate((q0, q1, q2, q3)):
        yy = lax.rem(spot[1] + 4 - k, 4)
        for side in range(2):
            zh = spot[0] if side == 0 else 1 - spot[0]
            acc = None
            for layer in range(3):
                part = dot_t(grads[:, layer * LANE : layer * LANE + LANE], ref[side, layer])
                acc = part if acc is None else acc + part
            for n in range(4):
                out[pl.ds((zh * 4 + yy) * 4 + n, 1), :] = acc[:, n * 64 : n * 64 + 64]


def embed_kernel(ids, clip, table, target, out, rows_buf):
    frames = ids.shape[1]
    per = clip.shape[0] // frames
    rows = out.shape[1]
    for f in range(frames):
        group = pl.multiple_of((ids[0, f] // 16) * 16, 16)
        at = ids[0, f] - group
        tile = table[pl.ds(group, 16), :].astype(F32)
        pick = lax.broadcasted_iota(jnp.int32, (16, 1), 0) == at
        row = jnp.sum(jnp.where(pick, tile, 0.0), axis=0, keepdims=True)
        rows_buf[f * per : f * per + per, :] = (clip[f * per : f * per + per, :].astype(F32) + row).astype(BF)
    for n in range(out.shape[0]):
        out[n, :, 0:LANE] = rows_buf[n * rows : n * rows + rows, :]
        out[n, :, LANE:] = target[n * rows : n * rows + rows, :]


def call(kernel, out_shape, in_specs, scratch, flops, moved, name, *args):
    many = isinstance(out_shape, (tuple, list))
    return pl.pallas_call(
        kernel,
        out_shape=out_shape,
        in_specs=in_specs,
        out_specs=[vmem() for _ in out_shape] if many else vmem(),
        scratch_shapes=scratch,
        compiler_params=pltpu.CompilerParams(vmem_limit_bytes=VLIMIT),
        cost_estimate=pl.CostEstimate(flops=1000, bytes_accessed=1000, transcendentals=0),
        name=name,
    )(*args)


def ring(x, axes, size, k):
    return lax.ppermute(x, axes, [(i, (i + k) % size) for i in range(size)])


def swap(x):
    return lax.ppermute(x, "c", [(0, 1), (1, 0)])


def zring(x, k):
    return ring(x, ("zh", "z"), 8, k)


def spread(x):
    return [x] + [ring(x, "x", 4, k) for k in (1, 2, 3)]


def after(x, *others):
    return lax.optimization_barrier((x, *others))[0]


def gather_over_y(own, *wait):
    quarter = own.shape[0] // 4
    mine = lax.dynamic_slice_in_dim(own, lax.axis_index("y") * quarter, quarter, 0)
    parts = [zring(mine, 1), zring(mine, -1), zring(mine, 2)]
    parts = [mine] + [after(part, *wait) for part in parts]
    packed = jnp.stack(parts)
    whole = lax.all_gather(packed, ("y", "c"))
    places = []
    for y in range(4):
        for slot in range(4):
            for core in range(2):
                places.append((("y", y, core, slot), 0, quarter, slot, y * quarter, core))
    return [whole] * len(places), places


class Gather:
    def __init__(self, own):
        self.own = own
        self.half = own.shape[0] // 2

    def first(self):
        self.right, self.left = zring(self.own, 1), zring(self.own, -1)
        self.swaps = [swap(self.own)]

    def second(self, *wait):
        right, left = self.right, self.left
        if wait:
            right, left = after(right, *wait), after(left, *wait)
        self.right2, self.left2 = zring(right[: self.half], 1), zring(left[self.half :], -1)
        self.swaps += [swap(right), swap(left)]

    def last(self, *wait):
        right2, left2 = self.right2, self.left2
        if wait:
            right2, left2 = after(right2, *wait), after(left2, *wait)
        self.swaps += [swap(right2), swap(left2)]
        half = self.half
        arrays, places = [], []
        own = [self.own, self.right, self.left, self.right2, self.left2]
        spots = [(0, 0), (1, 0), (2, 0), (3, 0), (3, half)]
        for side, group in enumerate((own, self.swaps)):
            for array, (slot, row) in zip(group, spots):
                arrays.append(array)
                places.append((None, 0, array.shape[0], slot, row, side))
        return arrays, places


def local(
    clip_tokens,
    action_ids,
    token_counts,
    action_table,
    norm_gain,
    layer_weight,
    in_factor,
    out_factor,
    query_grads,
    target,
):
    width = norm_gain.shape[1]
    rows = clip_tokens.shape[0] // 8
    meta = jnp.stack(
        [lax.axis_index("z"), lax.axis_index("x"), lax.axis_index("c"), token_counts[0]]
    ).astype(jnp.int32)
    block = lambda dtype: jax.ShapeDtypeStruct((8, rows, LANE), dtype)
    whole = jax.ShapeDtypeStruct((rows, width), BF)
    ratio_shape = jax.ShapeDtypeStruct((rows, LANE), F32)
    flops = 2 * rows * width * 1024
    moved = width * 1024 * 2

    factors = jnp.concatenate([in_factor[:, 0::2], in_factor[:, 1::2], out_factor], axis=1)
    tail = jnp.concatenate([layer_weight[2], factors.reshape(-1, LANE)], axis=0)
    g0 = Gather(layer_weight[0])
    g0.first()
    g0.second()
    w0 = g0.last()
    g2 = Gather(after(tail, g0.right, g0.left))
    g2.first()

    start = call(
        embed_kernel,
        jax.ShapeDtypeStruct((8, rows, 2 * LANE), BF),
        [smem(), vmem(), vmem(), vmem()],
        [pltpu.VMEM((8 * rows, LANE), BF)],
        10**6,
        10**6,
        "embed",
        action_ids,
        clip_tokens,
        action_table,
        target,
    )
    start = lax.all_to_all(start, ("z", "c"), 0, 0)
    state = start[:, :, :LANE]
    goal = start[:, :, LANE:]
    arrays1, places1 = gather_over_y(layer_weight[1], start)
    queries = jnp.stack([query_grads, lax.ppermute(query_grads, "zh", [(0, 1), (1, 0)])])
    queries = [queries] + [ring(queries, "y", 4, k) for k in (1, 2, 3)]

    def wscratch(places, height):
        return [pltpu.VMEM((4, height, 256), BF)], [pltpu.SemaphoreType.DMA((len(places),))]

    def forward(layer, state, weight):
        arrays, places = weight
        wb, sems = wscratch(places, width)
        blocks = spread(state)
        return call(
            functools.partial(forward_kernel, layer, places, width),
            [block(BF), block(F32), block(BF), whole, ratio_shape],
            [smem()] + [vmem()] * 5 + [hbm()] * len(places),
            wb + [pltpu.VMEM((rows, width), BF)] + sems,
            flops,
            moved,
            "forward%d" % layer,
            meta,
            *blocks,
            norm_gain,
            *arrays,
        )

    state, pre0, u0, _, _ = forward(0, state, w0)
    g2.second(state)
    w1 = arrays1, places1
    state, pre1, u1, hfull1, ratio1 = forward(1, state, w1)
    arrays, places = g2.last(state)

    wb, sems = wscratch(places, tail.shape[0])
    blocks = spread(state)
    delta, inner, q2, fout, *parts = call(
        functools.partial(turn_kernel, 2, places, width),
        [
            block(F32),
            jax.ShapeDtypeStruct((2, rows, LANE), F32),
            jax.ShapeDtypeStruct((rows, 64), F32),
            jax.ShapeDtypeStruct((2, 4, 64, 256), BF),
            block(F32),
        ]
        + [jax.ShapeDtypeStruct((10, rows, LANE), BF)] * 3,
        [smem()] + [vmem()] * 8 + [hbm()] * len(places),
        [
            pltpu.VMEM((8, rows, LANE), BF),
            pltpu.VMEM((8, rows, LANE), BF),
            pltpu.VMEM((rows, width), BF),
            pltpu.VMEM((rows, LANE), F32),
            pltpu.VMEM((8, rows, LANE), F32),
        ]
        + wb
        + [pltpu.VMEM((rows, width), BF)]
        + sems,
        2 * flops,
        moved,
        "turn",
        meta,
        *blocks,
        norm_gain,
        goal,
        u0,
        u1,
        *arrays,
    )

    def scatter(parts):
        return [parts[0]] + [ring(parts[k], "x", 4, k) for k in (1, 2, 3)]

    incs = scatter(parts)

    arrays, places = w1
    wb, sems = wscratch(places, width)
    delta, pfull, gpart, *parts = call(
        functools.partial(back_kernel, 1, places, width),
        [
            block(F32),
            jax.ShapeDtypeStruct((rows, 64), F32),
            jax.ShapeDtypeStruct((32, 256), F32),
            block(F32),
            block(BF),
            block(BF),
            block(BF),
        ],
        [smem()] + [vmem()] * 12 + [hbm()] * len(places),
        [pltpu.VMEM((8, rows, LANE), BF)] + wb + sems,
        flops,
        moved,
        "back1",
        meta,
        delta,
        *incs,
        pre1,
        hfull1,
        ratio1,
        norm_gain,
        fout,
        inner,
        q2,
        *arrays,
    )
    incs = scatter(parts)
    gall = call(
        last_kernel,
        jax.ShapeDtypeStruct((32, 384), F32),
        [smem()] + [vmem()] * 9,
        [pltpu.VMEM((8, rows, LANE), BF)],
        10**7,
        10**6,
        "last",
        meta,
        delta,
        *incs,
        pre0,
        fout,
        pfull,
        gpart,
    )
    everyone = ("z", "x", "c")
    gall = lax.all_to_all(gall, everyone, 0, 0, tiled=True)
    spot = jnp.stack([lax.axis_index("zh"), lax.axis_index("y")]).astype(jnp.int32)
    partial = call(
        score_kernel,
        jax.ShapeDtypeStruct((32, 64), F32),
        [smem()] + [vmem()] * 5,
        [],
        10**6,
        10**6,
        "score",
        spot,
        gall,
        *queries,
    )
    mine = lax.all_to_all(partial, everyone, 0, 0, tiled=True)
    return jnp.sum(mine, axis=0, keepdims=True)


def solution(mesh):
    fine = Mesh(mesh.devices.reshape(2, 4, 4, 4, 2), ("zh", "y", "z", "x", "c"))
    dp = ("zh", "y")
    fsdp = ("z", "x", "c")
    return jax.shard_map(
        local,
        mesh=fine,
        in_specs=(
            P(dp, fsdp),
            P(dp, None),
            P(dp),
            P(None, fsdp),
            P(),
            P(None, None, fsdp),
            P(None, None, fsdp),
            P(None, None, fsdp),
            P(None, dp, fsdp),
            P(dp, fsdp),
        ),
        out_specs=P(dp, fsdp),
        check_vma=False,
    )
```

```python
import functools

import jax
import jax.numpy as jnp
from jax import lax
from jax.experimental import pallas as pl
from jax.experimental.pallas import tpu as pltpu
from jax.sharding import Mesh, PartitionSpec as P

EPS = 1e-06
BF = jnp.bfloat16
F32 = jnp.float32
LANE = 128
VLIMIT = 8 * 1024 * 1024


def hbm():
    return pl.BlockSpec(memory_space=pltpu.HBM)


def vmem():
    return pl.BlockSpec(memory_space=pltpu.VMEM)


def smem():
    return pl.BlockSpec(memory_space=pltpu.SMEM)


def feature(zz, xx, cc):
    return pl.multiple_of(zz * 1024 + xx * 256 + cc * LANE, LANE)


SLOT_Z = (0, 3, 1, 2)


def load_weight(meta, places, refs, wbuf, sems):
    copies = []
    for n, (place, ref) in enumerate(zip(places, refs)):
        index, first, rows, slot, row, core = place
        if index is None:
            src = ref
        else:
            owner = meta[2] if core == 0 else 1 - meta[2]
            src = ref.at[index * 2 + owner, slot]
        copy = pltpu.make_async_copy(
            src.at[pl.ds(first, rows)],
            wbuf.at[slot, pl.ds(row, rows), pl.ds(core * LANE, LANE)],
            sems.at[n],
        )
        copy.start()
        copies.append((slot, copy))
    return copies


def assemble_kernel(places, meta, *rest):
    n = len(places)
    for slot, copy in load_weight(meta, places, rest[:n], rest[n], rest[n + 1]):
        copy.wait()


def assemble(meta, weight, height, name):
    arrays, places = weight
    held = pltpu.with_memory_space_constraint
    arrays = [held(x, pltpu.HBM) if x.ndim > 2 or p[5] else x for x, p in zip(arrays, places)]
    return pl.pallas_call(
        functools.partial(assemble_kernel, places),
        out_shape=pltpu.VMEM((4, height, 256), BF),
        in_specs=[smem()] + [hbm()] * len(places),
        out_specs=vmem(),
        scratch_shapes=[pltpu.SemaphoreType.DMA((len(places),))],
        compiler_params=pltpu.CompilerParams(vmem_limit_bytes=VLIMIT),
        cost_estimate=pl.CostEstimate(flops=1000, bytes_accessed=1000, transcendentals=0),
        name=name,
    )(meta, *arrays)


def block_of(meta, slot, core):
    zz = lax.rem(meta[0] + SLOT_Z[slot], 4)
    cc = meta[2] if core == 0 else 1 - meta[2]
    return zz * 2 + cc


def sigm(v):
    return 1.0 / (1.0 + jnp.exp(-v))


def norm_rows(meta, layer, blocks, gain, hfull, ubuf, width):
    total = None
    for k, ref in enumerate(blocks):
        xx = lax.rem(meta[1] + 4 - k, 4)
        for j in range(8):
            block = ref[j]
            hfull[:, pl.ds(feature(j // 2, xx, j % 2), LANE)] = block
            value = block.astype(F32)
            total = value * value if total is None else total + value * value
    ratio = lax.rsqrt(jnp.sum(total, axis=1, keepdims=True) / width + EPS)
    for n in range(width // 256):
        cols = slice(n * 256, n * 256 + 256)
        ubuf[:, cols] = (hfull[:, cols].astype(F32) * ratio * gain[layer : layer + 1, cols]).astype(BF)
    return ratio


def forward_body(meta, layer, blocks, gain, wbuf, hfull, rout, uown, aout, ubuf, width, finish):
    ratio = norm_rows(meta, layer, blocks, gain, hfull, ubuf, width)
    rout[...] = jnp.broadcast_to(ratio, rout.shape)
    for j in range(8):
        uown[j] = ubuf[:, pl.ds(feature(j // 2, meta[1], j % 2), LANE)]
    for slot in range(4):
        pre = jnp.dot(ubuf[...], wbuf[slot, 0:width, :], preferred_element_type=F32)
        for core in range(2):
            value = pre[:, core * LANE : core * LANE + LANE]
            j = block_of(meta, slot, core)
            aout[j] = value
            finish(j, value)
    return ratio


def forward_kernel(layer, width, meta, h0, h1, h2, h3, gain, wbuf, hnew, aout, uown, hfull, rout, ubuf):
    def finish(j, value):
        hnew[j] = (h0[j].astype(F32) + value * sigm(value)).astype(BF)

    forward_body(meta, layer, (h0, h1, h2, h3), gain, wbuf, hfull, rout, uown, aout, ubuf, width, finish)


def back_product(meta, layer, aref, eout, hfull, ratio, gain, wbuf, outs, width):
    dot_sum = None
    for j in range(8):
        term = eout[j].astype(F32) * aref[j]
        dot_sum = term if dot_sum is None else dot_sum + term
    scale = ratio * ratio * (jnp.sum(dot_sum, axis=1, keepdims=True) / width)
    grads = []
    for slot in range(4):
        grads.append(
            jnp.concatenate([eout[block_of(meta, slot, 0)], eout[block_of(meta, slot, 1)]], axis=1)
        )
    for k, out in enumerate(outs):
        xx = lax.rem(meta[1] + k, 4)
        for zz in range(4):
            first = pl.multiple_of(zz * 1024 + xx * 256, 256)
            acc = None
            for slot in range(4):
                part = lax.dot_general(
                    grads[slot],
                    wbuf[slot, pl.ds(first, 256), :],
                    (((1,), (1,)), ((), ())),
                    preferred_element_type=F32,
                )
                acc = part if acc is None else acc + part
            value = ratio * gain[layer : layer + 1, pl.ds(first, 256)] * acc - scale * hfull[
                :, pl.ds(first, 256)
            ].astype(F32)
            for cc in range(2):
                out[zz * 2 + cc] = value[:, cc * LANE : cc * LANE + LANE].astype(out.dtype)


def grad_of(delta, value):
    sig = sigm(value)
    return (delta * (sig * (1.0 + value * (1.0 - sig)))).astype(BF)


def factor_rows(width, layer, which):
    first = width + (layer * 2 + which) * 64
    return slice(first, first + 64)


def slot_pair(meta, ref, slot):
    return jnp.concatenate([ref[block_of(meta, slot, 0)], ref[block_of(meta, slot, 1)]], axis=1)


def turn_kernel(layer, width, meta, h0, h1, h2, h3, gain, target, u0, u1, wbuf, *rest):
    delta, pout, qout, fout, o0, o1, o2, o3, eout, uown, hfull, rout, aout, ubuf = rest
    rows = h0.shape[1]
    token = (meta[0] * 2 + meta[2]) * rows + lax.broadcasted_iota(jnp.int32, (rows, 1), 0)
    live = token < meta[3]

    def finish(j, value):
        hlast = (h0[j].astype(F32) + value * sigm(value)).astype(BF)
        grad = jnp.where(live, hlast.astype(F32) - target[j].astype(F32), 0.0)
        delta[j] = grad
        eout[j] = grad_of(grad, value)

    ratio = forward_body(
        meta, layer, (h0, h1, h2, h3), gain, wbuf, hfull, rout, uown, aout, ubuf, width, finish
    )
    back_product(meta, layer, aout, eout, hfull, ratio, gain, wbuf, (o0, o1, o2, o3), width)
    for at, ref in enumerate((u0, u1, uown)):
        acc = None
        for slot in range(4):
            part = dot_t(slot_pair(meta, ref, slot), wbuf[slot, factor_rows(width, at, 0), :])
            acc = part if acc is None else acc + part
        lanes = slice(at % 2 * 64, at % 2 * 64 + 64)
        pout[at // 2, :, lanes] = acc
        for out in (o1, o2, o3):
            out[8 + at // 2, :, lanes] = acc.astype(BF)
    for out in (o1, o2, o3):
        out[9, :, 64:] = jnp.zeros((rows, 64), BF)
    pout[1, :, 64:] = jnp.zeros((rows, 64), F32)
    acc = None
    for slot in range(4):
        part = dot_t(slot_pair(meta, eout, slot), wbuf[slot, factor_rows(width, 2, 1), :])
        acc = part if acc is None else acc + part
        for at in range(2):
            fout[at, slot] = wbuf[slot, factor_rows(width, at, 1), :]
    qout[...] = acc


def project(meta, eref, fref, layer):
    acc = None
    for slot in range(4):
        part = dot_t(slot_pair(meta, eref, slot), fref[layer, slot])
        acc = part if acc is None else acc + part
    return acc


def back_kernel(layer, width, meta, din, i0, i1, i2, i3, aref, hfull, rref, gain, fref, pin, q2, wbuf, *rest):
    delta, pout, gout, o0, o1, o2, o3, eout = rest
    for j in range(8):
        grad = din[j] + i0[j] + i1[j].astype(F32) + i2[j].astype(F32) + i3[j].astype(F32)
        delta[j] = grad
        eout[j] = grad_of(grad, aref[j])
    back_product(meta, layer, aref, eout, hfull, rref[:, 0:1], gain, wbuf, (o0, o1, o2, o3), width)
    psum = [
        pin[n] + i1[8 + n].astype(F32) + i2[8 + n].astype(F32) + i3[8 + n].astype(F32) for n in range(2)
    ]
    pout[...] = psum[0][:, 0:64]
    gout[:, 0:LANE] = outer(psum[0][:, 64:LANE], project(meta, eout, fref, 1))
    gout[:, LANE:] = outer(psum[1][:, 0:64], q2[...])


def dot_t(left, right):
    return lax.dot_general(left, right, (((1,), (1,)), ((), ())), preferred_element_type=F32)


def outer(left, right):
    full = lax.dot_general(
        left, right, (((0,), (0,)), ((), ())), preferred_element_type=F32, precision=lax.Precision.HIGHEST
    )
    return jnp.concatenate([full[:32], full[32:]], axis=1)


def last_kernel(meta, din, i0, i1, i2, i3, aref, fref, pref, gin, out, eout):
    for j in range(8):
        grad = din[j] + i0[j] + i1[j].astype(F32) + i2[j].astype(F32) + i3[j].astype(F32)
        eout[j] = grad_of(grad, aref[j])
    out[:, 0:LANE] = outer(pref[...], project(meta, eout, fref, 0))
    out[:, LANE:] = gin[...]


def score_kernel(gall, queries, out):
    grads = jnp.sum(gall[...], axis=0, keepdims=True).astype(BF)
    for d in range(queries.shape[0]):
        acc = None
        for layer in range(3):
            part = dot_t(grads[:, layer * LANE : layer * LANE + LANE], queries[d, layer])
            acc = part if acc is None else acc + part
        for n in range(4):
            out[d * 4 + n : d * 4 + n + 1, :] = acc[:, n * 64 : n * 64 + 64]


def embed_kernel(ids, clip, table, target, out, rows_buf):
    frames = ids.shape[1]
    per = clip.shape[0] // frames
    rows = out.shape[1]
    for f in range(frames):
        group = pl.multiple_of((ids[0, f] // 16) * 16, 16)
        at = ids[0, f] - group
        tile = table[pl.ds(group, 16), :].astype(F32)
        pick = lax.broadcasted_iota(jnp.int32, (16, 1), 0) == at
        row = jnp.sum(jnp.where(pick, tile, 0.0), axis=0, keepdims=True)
        rows_buf[f * per : f * per + per, :] = (clip[f * per : f * per + per, :].astype(F32) + row).astype(BF)
    for n in range(out.shape[0]):
        out[n, :, 0:LANE] = rows_buf[n * rows : n * rows + rows, :]
        out[n, :, LANE:] = target[n * rows : n * rows + rows, :]


def call(kernel, out_shape, in_specs, scratch, flops, moved, name, *args):
    many = isinstance(out_shape, (tuple, list))
    return pl.pallas_call(
        kernel,
        out_shape=out_shape,
        in_specs=in_specs,
        out_specs=[vmem() for _ in out_shape] if many else vmem(),
        scratch_shapes=scratch,
        compiler_params=pltpu.CompilerParams(vmem_limit_bytes=VLIMIT),
        cost_estimate=pl.CostEstimate(flops=1000, bytes_accessed=1000, transcendentals=0),
        name=name,
    )(*args)


def ring(x, axes, size, k):
    return lax.ppermute(x, axes, [(i, (i + k) % size) for i in range(size)])


def swap(x):
    return lax.ppermute(x, "c", [(0, 1), (1, 0)])


def zring(x, k):
    return ring(x, ("zh", "z"), 8, k)


def spread(x):
    return [x] + [ring(x, "x", 4, k) for k in (1, 2, 3)]


def after(x, *others):
    return lax.optimization_barrier((x, *others))[0]


def gather_over_y(own):
    quarter = own.shape[0] // 4
    mine = lax.dynamic_slice_in_dim(own, lax.axis_index("y") * quarter, quarter, 0)
    half = quarter // 2
    far = jnp.concatenate([zring(mine[:half], 2), zring(mine[half:], -2)])
    parts = [mine, zring(mine, 1), zring(mine, -1), far]
    packed = jnp.stack(parts)
    whole = lax.all_gather(packed, ("y", "c"))
    places = []
    for y in range(4):
        for slot in range(4):
            for core in range(2):
                places.append((y, 0, quarter, slot, y * quarter, core))
    return ([whole] * len(places), places), parts


def stage_kernel(cuts, *rest):
    refs, outs, sems = rest[: -len(cuts) - 1], rest[-len(cuts) - 1 : -1], rest[-1]
    copies = []
    for n, ((at, first, rows), out) in enumerate(zip(cuts, outs)):
        copies.append(pltpu.make_async_copy(refs[at].at[pl.ds(first, rows)], out, sems.at[n]))
        copies[-1].start()
    for copy in copies:
        copy.wait()


def stage(name, cuts, *arrays):
    return pl.pallas_call(
        functools.partial(stage_kernel, cuts),
        out_shape=[pltpu.VMEM((rows, LANE), BF) for _, _, rows in cuts],
        in_specs=[hbm()] * len(arrays),
        out_specs=[vmem() for _ in cuts],
        scratch_shapes=[pltpu.SemaphoreType.DMA((len(cuts),))],
        compiler_params=pltpu.CompilerParams(vmem_limit_bytes=VLIMIT),
        cost_estimate=pl.CostEstimate(flops=1000, bytes_accessed=1000, transcendentals=0),
        name=name,
    )(*[pltpu.with_memory_space_constraint(x, pltpu.HBM) for x in arrays])


class Gather:
    def __init__(self, own, name):
        self.rows, self.name = own.shape[0], name
        self.own, self.right, self.left = own, zring(own, 1), zring(own, -1)
        self.swapped = swap(own)

    def last(self, second=()):
        half = self.rows // 2
        right, left = self.right, self.left
        if second:
            right, left = after(right, *second), after(left, *second)
        right, left, rpart, lpart = stage(
            self.name + "a",
            ((0, 0, 2 * half), (1, 0, 2 * half), (0, 0, half), (1, half, half)),
            right,
            left,
        )
        right2, left2 = zring(rpart, 1), zring(lpart, -1)
        self.parts2 = [right2, left2]
        right2, left2 = stage(self.name + "b", ((0, 0, half), (1, 0, half)), right2, left2)
        mine = [self.own, right, left, right2, left2]
        other = [self.swapped] + [swap(part) for part in mine[1:]]
        spots = [(0, 0), (1, 0), (2, 0), (3, 0), (3, half)]
        arrays, places = [], []
        for side, group in enumerate((mine, other)):
            for array, (slot, row) in zip(group, spots):
                arrays.append(array)
                places.append((None, 0, array.shape[0], slot, row, side))
        return arrays, places


def local(
    clip_tokens,
    action_ids,
    token_counts,
    action_table,
    norm_gain,
    layer_weight,
    in_factor,
    out_factor,
    query_grads,
    target,
):
    width = norm_gain.shape[1]
    rows = clip_tokens.shape[0] // 8
    meta = jnp.stack(
        [lax.axis_index("z"), lax.axis_index("x"), lax.axis_index("c"), token_counts[0]]
    ).astype(jnp.int32)
    block = lambda dtype: jax.ShapeDtypeStruct((8, rows, LANE), dtype)
    whole = jax.ShapeDtypeStruct((rows, width), BF)
    ratio_shape = jax.ShapeDtypeStruct((rows, LANE), F32)
    flops = 2 * rows * width * 1024
    moved = width * 1024 * 2

    factors = jnp.concatenate([in_factor[:, 0::2], in_factor[:, 1::2], out_factor], axis=1)
    tail = jnp.concatenate([layer_weight[2], factors.reshape(-1, LANE)], axis=0)
    w1, first = gather_over_y(layer_weight[1])

    start = call(
        embed_kernel,
        jax.ShapeDtypeStruct((8, rows, 2 * LANE), BF),
        [smem(), vmem(), vmem(), vmem()],
        [pltpu.VMEM((8 * rows, LANE), BF)],
        10**6,
        10**6,
        "embed",
        action_ids,
        clip_tokens,
        action_table,
        target,
    )
    start = lax.all_to_all(start, ("z", "c"), 0, 0)
    state = start[:, :, :LANE]
    goal = start[:, :, LANE:]
    g0 = Gather(after(layer_weight[0], *first), "zero")
    g2 = Gather(after(tail, g0.right, g0.left), "two")
    w0 = g0.last((start,))

    def forward(layer, state, weight, *wait):
        blocks = spread(state)
        if wait:
            blocks[0] = after(blocks[0], *wait)
        return call(
            functools.partial(forward_kernel, layer, width),
            [block(BF), block(F32), block(BF), whole, ratio_shape],
            [smem()] + [vmem()] * 6,
            [pltpu.VMEM((rows, width), BF)],
            flops,
            moved,
            "forward%d" % layer,
            meta,
            *blocks,
            norm_gain,
            weight,
        )

    state, pre0, u0, _, _ = forward(0, state, assemble(meta, w0, width, "assemble0"), g2.right, g2.left)
    w2 = g2.last()
    w1 = assemble(meta, w1, width, "assemble1")
    state, pre1, u1, hfull1, ratio1 = forward(1, state, w1, *g2.parts2)
    queries = lax.all_gather(after(query_grads, state), ("zh", "y"))
    blocks = spread(state)
    w2 = assemble(meta, w2, tail.shape[0], "assemble2")
    delta, inner, q2, fout, *parts = call(
        functools.partial(turn_kernel, 2, width),
        [
            block(F32),
            jax.ShapeDtypeStruct((2, rows, LANE), F32),
            jax.ShapeDtypeStruct((rows, 64), F32),
            jax.ShapeDtypeStruct((2, 4, 64, 256), BF),
            block(F32),
        ]
        + [jax.ShapeDtypeStruct((10, rows, LANE), BF)] * 3,
        [smem()] + [vmem()] * 9,
        [
            pltpu.VMEM((8, rows, LANE), BF),
            pltpu.VMEM((8, rows, LANE), BF),
            pltpu.VMEM((rows, width), BF),
            pltpu.VMEM((rows, LANE), F32),
            pltpu.VMEM((8, rows, LANE), F32),
            pltpu.VMEM((rows, width), BF),
        ],
        2 * flops,
        moved,
        "turn",
        meta,
        *blocks,
        norm_gain,
        goal,
        u0,
        u1,
        w2,
    )

    def scatter(parts):
        return [parts[0]] + [ring(parts[k], "x", 4, k) for k in (1, 2, 3)]

    incs = scatter(parts)

    delta, pfull, gpart, *parts = call(
        functools.partial(back_kernel, 1, width),
        [
            block(F32),
            jax.ShapeDtypeStruct((rows, 64), F32),
            jax.ShapeDtypeStruct((32, 256), F32),
            block(F32),
            block(BF),
            block(BF),
            block(BF),
        ],
        [smem()] + [vmem()] * 13,
        [pltpu.VMEM((8, rows, LANE), BF)],
        flops,
        moved,
        "back1",
        meta,
        delta,
        *incs,
        pre1,
        hfull1,
        ratio1,
        norm_gain,
        fout,
        inner,
        q2,
        w1,
    )
    incs = scatter(parts)
    gall = call(
        last_kernel,
        jax.ShapeDtypeStruct((32, 384), F32),
        [smem()] + [vmem()] * 9,
        [pltpu.VMEM((8, rows, LANE), BF)],
        10**7,
        10**6,
        "last",
        meta,
        delta,
        *incs,
        pre0,
        fout,
        pfull,
        gpart,
    )
    everyone = ("z", "x", "c")
    gall = lax.all_to_all(gall, everyone, 0, 0, tiled=True)
    partial = call(
        score_kernel,
        jax.ShapeDtypeStruct((32, 64), F32),
        [vmem()] * 2,
        [],
        10**6,
        10**6,
        "score",
        gall,
        queries,
    )
    mine = lax.all_to_all(partial, everyone, 0, 0, tiled=True)
    return jnp.sum(mine, axis=0, keepdims=True)


def solution(mesh):
    fine = Mesh(mesh.devices.reshape(2, 4, 4, 4, 2), ("zh", "y", "z", "x", "c"))
    dp = ("zh", "y")
    fsdp = ("z", "x", "c")
    return jax.shard_map(
        local,
        mesh=fine,
        in_specs=(
            P(dp, fsdp),
            P(dp, None),
            P(dp),
            P(None, fsdp),
            P(),
            P(None, None, fsdp),
            P(None, None, fsdp),
            P(None, None, fsdp),
            P(None, dp, fsdp),
            P(dp, fsdp),
        ),
        out_specs=P(dp, fsdp),
        check_vma=False,
    )
```

```python
import functools

import jax
import jax.numpy as jnp
from jax import lax
from jax.experimental import pallas as pl
from jax.experimental.pallas import tpu as pltpu
from jax.sharding import Mesh, PartitionSpec as P

EPS = 1e-06
BF = jnp.bfloat16
F32 = jnp.float32
LANE = 128
VLIMIT = 8 * 1024 * 1024


def hbm():
    return pl.BlockSpec(memory_space=pltpu.HBM)


def vmem():
    return pl.BlockSpec(memory_space=pltpu.VMEM)


def smem():
    return pl.BlockSpec(memory_space=pltpu.SMEM)


def feature(zz, xx, cc):
    return pl.multiple_of(zz * 1024 + xx * 256 + cc * LANE, LANE)


SLOT_Z = (0, 3, 1, 2)


def load_weight(meta, places, refs, wbuf, sems):
    copies = []
    for n, (place, ref) in enumerate(zip(places, refs)):
        index, first, rows, slot, row, core = place
        if index is None:
            src = ref
        else:
            owner = meta[2] if core == 0 else 1 - meta[2]
            src = ref.at[index * 2 + owner, slot]
        copy = pltpu.make_async_copy(
            src.at[pl.ds(first, rows)],
            wbuf.at[slot, pl.ds(row, rows), pl.ds(core * LANE, LANE)],
            sems.at[n],
        )
        copy.start()
        copies.append((slot, copy))
    return copies


def assemble_kernel(places, meta, *rest):
    n = len(places)
    for slot, copy in load_weight(meta, places, rest[:n], rest[n], rest[n + 1]):
        copy.wait()


def assemble(meta, weight, height, name):
    arrays, places = weight
    held = pltpu.with_memory_space_constraint
    arrays = [held(x, pltpu.HBM) if x.ndim > 2 or p[5] else x for x, p in zip(arrays, places)]
    return pl.pallas_call(
        functools.partial(assemble_kernel, places),
        out_shape=pltpu.VMEM((4, height, 256), BF),
        in_specs=[smem()] + [hbm()] * len(places),
        out_specs=vmem(),
        scratch_shapes=[pltpu.SemaphoreType.DMA((len(places),))],
        compiler_params=pltpu.CompilerParams(vmem_limit_bytes=VLIMIT),
        cost_estimate=pl.CostEstimate(flops=1000, bytes_accessed=1000, transcendentals=0),
        name=name,
    )(meta, *arrays)


def block_of(meta, slot, core):
    zz = lax.rem(meta[0] + SLOT_Z[slot], 4)
    cc = meta[2] if core == 0 else 1 - meta[2]
    return zz * 2 + cc


def sigm(v):
    return 1.0 / (1.0 + jnp.exp(-v))


def norm_rows(meta, layer, blocks, gain, hfull, ubuf, width):
    total = None
    for k, ref in enumerate(blocks):
        xx = lax.rem(meta[1] + 4 - k, 4)
        for j in range(8):
            block = ref[j]
            hfull[:, pl.ds(feature(j // 2, xx, j % 2), LANE)] = block
            value = block.astype(F32)
            total = value * value if total is None else total + value * value
    ratio = lax.rsqrt(jnp.sum(total, axis=1, keepdims=True) / width + EPS)
    for n in range(width // 256):
        cols = slice(n * 256, n * 256 + 256)
        ubuf[:, cols] = (hfull[:, cols].astype(F32) * ratio * gain[layer : layer + 1, cols]).astype(BF)
    return ratio


def forward_body(meta, layer, blocks, gain, wbuf, hfull, rout, uown, aout, ubuf, width, finish):
    ratio = norm_rows(meta, layer, blocks, gain, hfull, ubuf, width)
    rout[...] = jnp.broadcast_to(ratio, rout.shape)
    for j in range(8):
        uown[j] = ubuf[:, pl.ds(feature(j // 2, meta[1], j % 2), LANE)]
    for slot in range(4):
        pre = jnp.dot(ubuf[...], wbuf[slot, 0:width, :], preferred_element_type=F32)
        for core in range(2):
            value = pre[:, core * LANE : core * LANE + LANE]
            j = block_of(meta, slot, core)
            aout[j] = value
            finish(j, value)
    return ratio


def forward_kernel(layer, width, meta, h0, h1, h2, h3, gain, wbuf, hnew, aout, uown, hfull, rout, ubuf):
    def finish(j, value):
        hnew[j] = (h0[j].astype(F32) + value * sigm(value)).astype(BF)

    forward_body(meta, layer, (h0, h1, h2, h3), gain, wbuf, hfull, rout, uown, aout, ubuf, width, finish)


def back_product(meta, layer, aref, eout, hfull, ratio, gain, wbuf, outs, width):
    dot_sum = None
    for j in range(8):
        term = eout[j].astype(F32) * aref[j]
        dot_sum = term if dot_sum is None else dot_sum + term
    scale = ratio * ratio * (jnp.sum(dot_sum, axis=1, keepdims=True) / width)
    grads = []
    for slot in range(4):
        grads.append(
            jnp.concatenate([eout[block_of(meta, slot, 0)], eout[block_of(meta, slot, 1)]], axis=1)
        )
    for k, out in enumerate(outs):
        xx = lax.rem(meta[1] + k, 4)
        for zz in range(4):
            first = pl.multiple_of(zz * 1024 + xx * 256, 256)
            acc = None
            for slot in range(4):
                part = lax.dot_general(
                    grads[slot],
                    wbuf[slot, pl.ds(first, 256), :],
                    (((1,), (1,)), ((), ())),
                    preferred_element_type=F32,
                )
                acc = part if acc is None else acc + part
            value = ratio * gain[layer : layer + 1, pl.ds(first, 256)] * acc - scale * hfull[
                :, pl.ds(first, 256)
            ].astype(F32)
            for cc in range(2):
                out[zz * 2 + cc] = value[:, cc * LANE : cc * LANE + LANE].astype(out.dtype)


def grad_of(delta, value):
    sig = sigm(value)
    return (delta * (sig * (1.0 + value * (1.0 - sig)))).astype(BF)


def factor_rows(width, layer, which):
    first = width + (layer * 2 + which) * 64
    return slice(first, first + 64)


def slot_pair(meta, ref, slot):
    return jnp.concatenate([ref[block_of(meta, slot, 0)], ref[block_of(meta, slot, 1)]], axis=1)


def turn_kernel(layer, width, meta, h0, h1, h2, h3, gain, target, u0, u1, wbuf, *rest):
    delta, pout, qout, fout, o0, o1, o2, o3, eout, uown, hfull, rout, aout, ubuf = rest
    rows = h0.shape[1]
    token = (meta[0] * 2 + meta[2]) * rows + lax.broadcasted_iota(jnp.int32, (rows, 1), 0)
    live = token < meta[3]

    def finish(j, value):
        hlast = (h0[j].astype(F32) + value * sigm(value)).astype(BF)
        grad = jnp.where(live, hlast.astype(F32) - target[j].astype(F32), 0.0)
        delta[j] = grad
        eout[j] = grad_of(grad, value)

    ratio = forward_body(
        meta, layer, (h0, h1, h2, h3), gain, wbuf, hfull, rout, uown, aout, ubuf, width, finish
    )
    back_product(meta, layer, aout, eout, hfull, ratio, gain, wbuf, (o0, o1, o2, o3), width)
    for at, ref in enumerate((u0, u1, uown)):
        acc = None
        for slot in range(4):
            part = dot_t(slot_pair(meta, ref, slot), wbuf[slot, factor_rows(width, at, 0), :])
            acc = part if acc is None else acc + part
        lanes = slice(at % 2 * 64, at % 2 * 64 + 64)
        pout[at // 2, :, lanes] = acc
        for out in (o1, o2, o3):
            out[8 + at // 2, :, lanes] = acc.astype(BF)
    for out in (o1, o2, o3):
        out[9, :, 64:] = jnp.zeros((rows, 64), BF)
    pout[1, :, 64:] = jnp.zeros((rows, 64), F32)
    acc = None
    for slot in range(4):
        part = dot_t(slot_pair(meta, eout, slot), wbuf[slot, factor_rows(width, 2, 1), :])
        acc = part if acc is None else acc + part
        for at in range(2):
            fout[at, slot] = wbuf[slot, factor_rows(width, at, 1), :]
    qout[...] = acc


def project(meta, eref, fref, layer):
    acc = None
    for slot in range(4):
        part = dot_t(slot_pair(meta, eref, slot), fref[layer, slot])
        acc = part if acc is None else acc + part
    return acc


def back_kernel(layer, width, meta, din, i0, i1, i2, i3, aref, hfull, rref, gain, fref, pin, q2, wbuf, *rest):
    delta, pout, gout, o0, o1, o2, o3, eout = rest
    for j in range(8):
        grad = din[j] + i0[j] + i1[j].astype(F32) + i2[j].astype(F32) + i3[j].astype(F32)
        delta[j] = grad
        eout[j] = grad_of(grad, aref[j])
    back_product(meta, layer, aref, eout, hfull, rref[:, 0:1], gain, wbuf, (o0, o1, o2, o3), width)
    psum = [
        pin[n] + i1[8 + n].astype(F32) + i2[8 + n].astype(F32) + i3[8 + n].astype(F32) for n in range(2)
    ]
    pout[...] = psum[0][:, 0:64]
    gout[:, 0:LANE] = outer(psum[0][:, 64:LANE], project(meta, eout, fref, 1))
    gout[:, LANE:] = outer(psum[1][:, 0:64], q2[...])


def dot_t(left, right):
    return lax.dot_general(left, right, (((1,), (1,)), ((), ())), preferred_element_type=F32)


def outer(left, right):
    full = lax.dot_general(
        left, right, (((0,), (0,)), ((), ())), preferred_element_type=F32, precision=lax.Precision.HIGHEST
    )
    return jnp.concatenate([full[:32], full[32:]], axis=1)


def last_kernel(meta, din, i0, i1, i2, i3, aref, fref, pref, gin, out, eout):
    for j in range(8):
        grad = din[j] + i0[j] + i1[j].astype(F32) + i2[j].astype(F32) + i3[j].astype(F32)
        eout[j] = grad_of(grad, aref[j])
    out[:, 0:LANE] = outer(pref[...], project(meta, eout, fref, 0))
    out[:, LANE:] = gin[...]


def score_kernel(gall, queries, out):
    grads = jnp.sum(gall[...], axis=0, keepdims=True).astype(BF)
    for d in range(queries.shape[0]):
        acc = None
        for layer in range(3):
            part = dot_t(grads[:, layer * LANE : layer * LANE + LANE], queries[d, layer])
            acc = part if acc is None else acc + part
        for n in range(4):
            out[d * 4 + n : d * 4 + n + 1, :] = acc[:, n * 64 : n * 64 + 64]


def embed_kernel(ids, clip, table, target, out, rows_buf):
    frames = ids.shape[1]
    per = clip.shape[0] // frames
    rows = out.shape[1]
    for f in range(frames):
        group = pl.multiple_of((ids[0, f] // 16) * 16, 16)
        at = ids[0, f] - group
        tile = table[pl.ds(group, 16), :].astype(F32)
        pick = lax.broadcasted_iota(jnp.int32, (16, 1), 0) == at
        row = jnp.sum(jnp.where(pick, tile, 0.0), axis=0, keepdims=True)
        rows_buf[f * per : f * per + per, :] = (clip[f * per : f * per + per, :].astype(F32) + row).astype(BF)
    for n in range(out.shape[0]):
        out[n, :, 0:LANE] = rows_buf[n * rows : n * rows + rows, :]
        out[n, :, LANE:] = target[n * rows : n * rows + rows, :]


def call(kernel, out_shape, in_specs, scratch, flops, moved, name, *args):
    many = isinstance(out_shape, (tuple, list))
    return pl.pallas_call(
        kernel,
        out_shape=out_shape,
        in_specs=in_specs,
        out_specs=[vmem() for _ in out_shape] if many else vmem(),
        scratch_shapes=scratch,
        compiler_params=pltpu.CompilerParams(vmem_limit_bytes=VLIMIT),
        cost_estimate=pl.CostEstimate(flops=1000, bytes_accessed=1000, transcendentals=0),
        name=name,
    )(*args)


def ring(x, axes, size, k):
    return lax.ppermute(x, axes, [(i, (i + k) % size) for i in range(size)])


def swap(x):
    return lax.ppermute(x, "c", [(0, 1), (1, 0)])


def zring(x, k):
    return ring(x, ("zh", "z"), 8, k)


def spread(x):
    return [x] + [ring(x, "x", 4, k) for k in (1, 2, 3)]


def after(x, *others):
    return lax.optimization_barrier((x, *others))[0]


def gather_over_y(own):
    quarter = own.shape[0] // 4
    mine = lax.dynamic_slice_in_dim(own, lax.axis_index("y") * quarter, quarter, 0)
    half = quarter // 2
    far = jnp.concatenate([zring(mine[:half], 2), zring(mine[half:], -2)])
    parts = [mine, zring(mine, 1), zring(mine, -1), far]
    packed = jnp.stack(parts)
    whole = lax.all_gather(packed, ("y", "c"))
    places = []
    for y in range(4):
        for slot in range(4):
            for core in range(2):
                places.append((y, 0, quarter, slot, y * quarter, core))
    return ([whole] * len(places), places), parts


def stage_kernel(cuts, *rest):
    refs, outs, sems = rest[: -len(cuts) - 1], rest[-len(cuts) - 1 : -1], rest[-1]
    copies = []
    for n, ((at, first, rows), out) in enumerate(zip(cuts, outs)):
        copies.append(pltpu.make_async_copy(refs[at].at[pl.ds(first, rows)], out, sems.at[n]))
        copies[-1].start()
    for copy in copies:
        copy.wait()


def stage(name, cuts, *arrays):
    return pl.pallas_call(
        functools.partial(stage_kernel, cuts),
        out_shape=[pltpu.VMEM((rows, LANE), BF) for _, _, rows in cuts],
        in_specs=[hbm()] * len(arrays),
        out_specs=[vmem() for _ in cuts],
        scratch_shapes=[pltpu.SemaphoreType.DMA((len(cuts),))],
        compiler_params=pltpu.CompilerParams(vmem_limit_bytes=VLIMIT),
        cost_estimate=pl.CostEstimate(flops=1000, bytes_accessed=1000, transcendentals=0),
        name=name,
    )(*[pltpu.with_memory_space_constraint(x, pltpu.HBM) for x in arrays])


class Gather:
    def __init__(self, own, name):
        self.rows, self.name = own.shape[0], name
        self.own, self.right, self.left = own, zring(own, 1), zring(own, -1)
        self.swapped = swap(own)

    def last(self, second=(), third=()):
        half = self.rows // 2
        right, left = self.right, self.left
        if second:
            right, left = after(right, *second), after(left, *second)
        right, left, rpart, lpart = stage(
            self.name + "a",
            ((0, 0, 2 * half), (1, 0, 2 * half), (0, 0, half), (1, half, half)),
            right,
            left,
        )
        right2, left2 = zring(rpart, 1), zring(lpart, -1)
        self.parts2 = [right2, left2]
        if third:
            right2, left2 = after(right2, *third), after(left2, *third)
        right2, left2 = stage(self.name + "b", ((0, 0, half), (1, 0, half)), right2, left2)
        mine = [self.own, right, left, right2, left2]
        other = [self.swapped] + [swap(part) for part in mine[1:]]
        spots = [(0, 0), (1, 0), (2, 0), (3, 0), (3, half)]
        arrays, places = [], []
        for side, group in enumerate((mine, other)):
            for array, (slot, row) in zip(group, spots):
                arrays.append(array)
                places.append((None, 0, array.shape[0], slot, row, side))
        return arrays, places


def local(
    clip_tokens,
    action_ids,
    token_counts,
    action_table,
    norm_gain,
    layer_weight,
    in_factor,
    out_factor,
    query_grads,
    target,
):
    width = norm_gain.shape[1]
    rows = clip_tokens.shape[0] // 8
    meta = jnp.stack(
        [lax.axis_index("z"), lax.axis_index("x"), lax.axis_index("c"), token_counts[0]]
    ).astype(jnp.int32)
    block = lambda dtype: jax.ShapeDtypeStruct((8, rows, LANE), dtype)
    whole = jax.ShapeDtypeStruct((rows, width), BF)
    ratio_shape = jax.ShapeDtypeStruct((rows, LANE), F32)
    flops = 2 * rows * width * 1024
    moved = width * 1024 * 2

    factors = jnp.concatenate([in_factor[:, 0::2], in_factor[:, 1::2], out_factor], axis=1)
    tail = jnp.concatenate([layer_weight[2], factors.reshape(-1, LANE)], axis=0)
    w1, first = gather_over_y(layer_weight[1])

    start = call(
        embed_kernel,
        jax.ShapeDtypeStruct((8, rows, 2 * LANE), BF),
        [smem(), vmem(), vmem(), vmem()],
        [pltpu.VMEM((8 * rows, LANE), BF)],
        10**6,
        10**6,
        "embed",
        action_ids,
        clip_tokens,
        action_table,
        target,
    )
    start = lax.all_to_all(start, ("z", "c"), 0, 0)
    state = start[:, :, :LANE]
    goal = start[:, :, LANE:]
    g0 = Gather(after(layer_weight[0], *first), "zero")
    g2 = Gather(after(tail, g0.right, g0.left), "two")
    w0 = g0.last((start,))

    def forward(layer, state, weight, *wait):
        blocks = spread(state)
        if wait:
            blocks[0] = after(blocks[0], *wait)
        return call(
            functools.partial(forward_kernel, layer, width),
            [block(BF), block(F32), block(BF), whole, ratio_shape],
            [smem()] + [vmem()] * 6,
            [pltpu.VMEM((rows, width), BF)],
            flops,
            moved,
            "forward%d" % layer,
            meta,
            *blocks,
            norm_gain,
            weight,
        )

    state, pre0, u0, _, _ = forward(0, state, assemble(meta, w0, width, "assemble0"))
    after0 = state
    w1 = assemble(meta, w1, width, "assemble1")
    state, pre1, u1, hfull1, ratio1 = forward(1, state, w1)
    blocks = spread(state)
    w2 = g2.last((after0,), blocks[1:])
    queries = lax.all_gather(after(query_grads, *blocks[1:]), ("zh", "y"))
    w2 = assemble(meta, w2, tail.shape[0], "assemble2")
    delta, inner, q2, fout, *parts = call(
        functools.partial(turn_kernel, 2, width),
        [
            block(F32),
            jax.ShapeDtypeStruct((2, rows, LANE), F32),
            jax.ShapeDtypeStruct((rows, 64), F32),
            jax.ShapeDtypeStruct((2, 4, 64, 256), BF),
            block(F32),
        ]
        + [jax.ShapeDtypeStruct((10, rows, LANE), BF)] * 3,
        [smem()] + [vmem()] * 9,
        [
            pltpu.VMEM((8, rows, LANE), BF),
            pltpu.VMEM((8, rows, LANE), BF),
            pltpu.VMEM((rows, width), BF),
            pltpu.VMEM((rows, LANE), F32),
            pltpu.VMEM((8, rows, LANE), F32),
            pltpu.VMEM((rows, width), BF),
        ],
        2 * flops,
        moved,
        "turn",
        meta,
        *blocks,
        norm_gain,
        goal,
        u0,
        u1,
        w2,
    )

    def scatter(parts):
        return [parts[0]] + [ring(parts[k], "x", 4, k) for k in (1, 2, 3)]

    incs = scatter(parts)

    delta, pfull, gpart, *parts = call(
        functools.partial(back_kernel, 1, width),
        [
            block(F32),
            jax.ShapeDtypeStruct((rows, 64), F32),
            jax.ShapeDtypeStruct((32, 256), F32),
            block(F32),
            block(BF),
            block(BF),
            block(BF),
        ],
        [smem()] + [vmem()] * 13,
        [pltpu.VMEM((8, rows, LANE), BF)],
        flops,
        moved,
        "back1",
        meta,
        delta,
        *incs,
        pre1,
        hfull1,
        ratio1,
        norm_gain,
        fout,
        inner,
        q2,
        w1,
    )
    incs = scatter(parts)
    gall = call(
        last_kernel,
        jax.ShapeDtypeStruct((32, 384), F32),
        [smem()] + [vmem()] * 9,
        [pltpu.VMEM((8, rows, LANE), BF)],
        10**7,
        10**6,
        "last",
        meta,
        delta,
        *incs,
        pre0,
        fout,
        pfull,
        gpart,
    )
    everyone = ("z", "x", "c")
    gall = lax.all_to_all(gall, everyone, 0, 0, tiled=True)
    partial = call(
        score_kernel,
        jax.ShapeDtypeStruct((32, 64), F32),
        [vmem()] * 2,
        [],
        10**6,
        10**6,
        "score",
        gall,
        queries,
    )
    mine = lax.all_to_all(partial, everyone, 0, 0, tiled=True)
    return jnp.sum(mine, axis=0, keepdims=True)


def solution(mesh):
    fine = Mesh(mesh.devices.reshape(2, 4, 4, 4, 2), ("zh", "y", "z", "x", "c"))
    dp = ("zh", "y")
    fsdp = ("z", "x", "c")
    return jax.shard_map(
        local,
        mesh=fine,
        in_specs=(
            P(dp, fsdp),
            P(dp, None),
            P(dp),
            P(None, fsdp),
            P(),
            P(None, None, fsdp),
            P(None, None, fsdp),
            P(None, None, fsdp),
            P(None, dp, fsdp),
            P(dp, fsdp),
        ),
        out_specs=P(dp, fsdp),
        check_vma=False,
    )
```
